32 devices in a mesh: groups: 2 (over y), feat: 4 (over z), dp: 2 (over x), rep: 2 (over core).
Axes of the slice: x: 2, y: 2, z: 4, core: 2. Of those that a mesh axis runs over, the one named last changes fastest.
Arguments:
- features: bfloat16 [8, 4096, 768], P(('groups', 'dp', 'rep'), None, 'feat'), parts along dimension 0, may hold values from -6 to 6
- self_ids: int32 [8, 512], P(('groups', 'dp', 'rep')), parts along dimension 0, may hold values from 0 to 4095
- first_dst: int32 [8, 6], P(('groups', 'dp', 'rep')), parts along dimension 0, may hold values from 0 to 3
- first_src: int32 [8, 6], P(('groups', 'dp', 'rep')), parts along dimension 0, may hold values from 0 to 31
- first_words: int32 [8, 6, 5, 128], P(('groups', 'dp', 'rep')), parts along dimension 0, may hold values from 0 to 1073741823, as said below
- second_dst: int32 [8, 5, 1], P(('groups', 'dp', 'rep')), parts along dimension 0, may hold values from 0 to 3; in each aligned block of 5 rows (0 to 4, 5 to 9, ..., all dimensions but the last counted through in order) at most 4 rows name the same one
- second_src: int32 [8, 5], P(('groups', 'dp', 'rep')), parts along dimension 0, may hold values from 0 to 3
- second_words: int32 [8, 5, 5, 128], P(('groups', 'dp', 'rep')), parts along dimension 0, may hold values from 0 to 1073741823, as said below
- w1_self: bfloat16 [768, 1024], P('feat'), may hold values from -0.21875 to 0.21875
- w1_neigh: bfloat16 [768, 1024], P('feat'), may hold values from -0.21875 to 0.21875
- bias_one: float32 [1024], replicated, may hold values from -3 to 3
- w2_self: bfloat16 [1024, 153], replicated, may hold values from -0.1875 to 0.1875
- w2_neigh: bfloat16 [1024, 153], replicated, may hold values from -0.1875 to 0.1875
- bias_two: float32 [153], replicated, may hold values from -3 to 3
- cotangent: float32 [8, 512, 153], P(('groups', 'dp', 'rep'), 'feat'), parts along dimension 0, may hold values from -0.06 to 0.06
Outputs:
- logits: float32 [8, 512, 153], P(('groups', 'dp', 'rep'), 'feat'), parts along dimension 0
- grad_self: float32 [2048, 153], P('groups'), parts along dimension 0
- grad_neigh: float32 [2048, 153], P('groups'), parts along dimension 0
The draws below stay inside these ranges and needn't reach their ends.
There are 2 independent parts, one for each index of `groups`. The reference program is written for one: setup_inputs(seed, part) draws one part's arguments, and reference() takes and returns one part's arrays. A program takes and returns all parts, laid end to end along the dimension named above; an argument that names none is the same for every part. Nothing has to cross between parts.
Inputs may be any that keep to these rules, and one draw needn't show every extreme that they name: `first_words`: bits for destination rows 128 and above (word 4, bits 8 to 29) are zero. `second_words`: bits for destination rows 128 and above (word 4, bits 8 to 29) are zero. `second_dst`: among the 5 tiles of one slot no destination block is named more than 4 times; in some slot a block is named exactly 4 times.
All inputs are finite; a program needn't handle non-finite values.
Results may differ from the reference program's by a relative error of at most 0.01.
Values may be sent and summed in bfloat16 or wider, within the bound.
A program may use at most 64 MiB of HBM per device.

```python
import math
import jax
import jax.numpy as jnp
import numpy as np
from jax import lax

F = 768
H = 1024
C = 153
BLK = 128
TMAX2 = 4
SRC_BLOCKS = 32
SLOTS = 4
COLS = 192
NODES = 512
SOURCES = 4096
TILE1 = 6
TILE2 = 5
N_FEAT = 4


def packed_masks(key, tile_count):
    key_level, key_fill = jax.random.split(key)
    levels = jax.random.randint(key_level, (SLOTS, tile_count, 150, 1), 1, 9)
    limits = jnp.left_shift(jnp.ones_like(levels), levels)
    fill_draws = jax.random.randint(key_fill, (SLOTS, tile_count, 150, BLK), 0, 1024)
    row_index = jnp.arange(150, dtype=jnp.int32)[None, None, :, None]
    bit_table = jnp.where((fill_draws < limits) & (row_index < BLK), 1, 0).astype(jnp.int32)
    shifts = jnp.arange(30, dtype=jnp.int32)[None, None, None, :, None]
    shifted = jnp.left_shift(bit_table.reshape(SLOTS, tile_count, 5, 30, BLK), shifts)
    return jnp.sum(shifted, axis=3).astype(jnp.int32)


def draw_first_words(key, part):
    key = jax.random.fold_in(key, 11)
    return packed_masks(key, TILE1)


def draw_second_words(key, part):
    key = jax.random.fold_in(key, 12)
    return packed_masks(key, TILE2)


def place_ends(entries, stream_key, low, high):
    place = [jax.random.randint(jax.random.fold_in(stream_key, axis), (), 0, length) for axis, length in enumerate(entries.shape)]
    widest = entries.shape.index(max(entries.shape))
    beside = place[:widest] + [(place[widest] + 1) % entries.shape[widest]] + place[widest + 1:]
    return entries.at[tuple(place)].set(low).at[tuple(beside)].set(high)


def block_scale(own_key, dims, shards, smallest, largest):
    gain, own = 1.0, jax.random.fold_in(own_key, 6)
    for dim, shards_of in shards:
        draws = jnp.exp(jax.random.uniform(jax.random.fold_in(own, dim), (shards_of,), jnp.float32, smallest / len(shards), largest / len(shards)))
        gain = gain * jnp.repeat(draws, dims[dim] // shards_of).reshape([-1 if axis == dim else 1 for axis in range(len(dims))])
    return gain


def cumulative_ranks(amount, slope):
    portions = [(1 << 20) // math.isqrt(standing ** slope) + 1 for standing in range(1, amount + 1)]
    scale = 1 + sum(portions) // (1 << 30)
    return np.cumsum(np.array([max(1, weight // scale) for weight in portions]))


def ranked_ids(stream_key, extent, number_of, skew):
    table = cumulative_ranks(number_of, skew)
    lot = jax.random.randint(jax.random.fold_in(stream_key, 1), extent, 0, int(table[number_of - 1]))
    grade = jnp.searchsorted(jnp.asarray(table, jnp.int32), lot, side="right")
    return jax.random.permutation(jax.random.fold_in(stream_key, 2), number_of)[grade].astype(jnp.int32)


def deal_out(key, own, number, rows, number_of, top, bound, skew):
    order = jax.random.permutation(key, number_of)
    packed, ordinary = shares(number_of, rows * top, bound, skew, True), shares(number_of, rows * top, bound, skew, False)
    places = jnp.arange(number_of)

    def named(tallies, offset_by):
        used = int((tallies > 0).sum())
        fixed = max(1, used // 4)
        moved = fixed + (places - fixed + offset_by * (used - fixed)) % max(1, number_of - fixed)
        return jnp.zeros((number_of,), jnp.int32).at[order[jnp.where(places < fixed, places, moved)]].set(jnp.asarray(tallies, jnp.int32))

    tallies = jnp.where(number % 4 == 0, named(packed, number // 4), named(ordinary, number - number // 4 - 1))
    mixed = jax.random.permutation(jax.random.fold_in(own, 3), number_of)
    source_of, taker = mixed[0:number_of // 2 * 2:2], mixed[1:number_of // 2 * 2:2]
    margin = jnp.minimum(tallies[source_of] - 1, bound - tallies[taker]) // 2
    margin = jnp.where((source_of == order[0]) | (taker == order[0]) | (tallies[taker] == 0), 0, jnp.maximum(margin, 0))
    moved = jax.random.randint(jax.random.fold_in(own, 4), (number_of // 2,), 0, 1 << 20) % (margin + 1)
    tallies = tallies.at[source_of].add(-moved).at[taker].add(moved)
    members = jnp.searchsorted(jnp.cumsum(tallies), jnp.arange(rows * top), side="right").astype(jnp.int32)
    listing = members.reshape(top, rows).T
    listing = listing[jax.random.permutation(jax.random.fold_in(own, 1), rows)]
    offset_by = jax.random.randint(jax.random.fold_in(own, 2), (rows, 1), 0, top)
    return jnp.take_along_axis(listing, (jnp.arange(top)[None, :] + offset_by) % top, axis=1)


def shares(amount, total, most, lean, full):
    portions = [(1 << 20) // math.isqrt(rank ** lean) + 1 for rank in range(1, amount + 1)]
    largest = most if full else min(most, max(-(-total // amount), total * portions[0] // sum(portions)))
    least = 1 if total - largest >= amount - 1 else 0
    counts, surplus = [largest] + [least] * (amount - 1), total - largest - least * (amount - 1)
    while surplus > 0:
        movable = [i for i in range(1, amount) if counts[i] < largest] or [i for i in range(1, amount) if counts[i] < most]
        whole, left = sum([portions[i] for i in movable]), surplus
        for i in movable:
            addition = min(most - counts[i], max(1, left * portions[i] // whole), surplus)
            counts[i] = counts[i] + addition
            surplus = surplus - addition
    return np.array(counts)


def bell_draw(stream_key, dims, spread, limit, pieces=(), kind=jnp.bfloat16):
    gain = block_scale(stream_key, dims, pieces, -0.22, 0.18) if pieces else 1.0
    entries = jax.random.normal(stream_key, dims, jnp.float32) * spread * gain
    return jnp.minimum(jnp.maximum(entries, -limit), limit).astype(kind)


def setup_inputs(seed: int = 0, part: int = 0) -> dict:
    key_of = jax.random.split(jax.random.key(seed), 16)
    own_keys = jax.random.split(jax.random.fold_in(key_of[15], part), 16)
    features = bell_draw(own_keys[0], (SLOTS, SOURCES, F), 1.0, 6.0, ((0, 4), (2, 4)))
    self_ids = place_ends(jax.random.randint(own_keys[1], (SLOTS, NODES), 0, SOURCES), jax.random.fold_in(own_keys[1], 1), 0, SOURCES - 1).astype(jnp.int32)
    first_dst = place_ends(ranked_ids(own_keys[2], (SLOTS, TILE1), N_FEAT, 2), jax.random.fold_in(own_keys[2], 3), 0, N_FEAT - 1).astype(jnp.int32)
    first_src = place_ends(jax.random.randint(own_keys[3], (SLOTS, TILE1), 0, SRC_BLOCKS), jax.random.fold_in(own_keys[3], 1), 0, SRC_BLOCKS - 1).astype(jnp.int32)
    first_words = draw_first_words(jax.random.fold_in(jax.random.fold_in(key_of[15], part), 71), part)
    second_dst_keys = jax.random.split(jax.random.fold_in(own_keys[5], 1), SLOTS * TILE2 // TILE2)
    second_dst_turns = jax.random.permutation(jax.random.fold_in(own_keys[5], 3), SLOTS * TILE2 // TILE2)
    second_dst = jax.vmap(lambda own, number: deal_out(jax.random.fold_in(own_keys[5], 2), own, number, TILE2, N_FEAT, 1, TMAX2, 2))(second_dst_keys, second_dst_turns).reshape((SLOTS, TILE2, 1))
    second_src = place_ends(jax.random.randint(own_keys[6], (SLOTS, TILE2), 0, N_FEAT), jax.random.fold_in(own_keys[6], 1), 0, N_FEAT - 1).astype(jnp.int32)
    second_words = draw_second_words(jax.random.fold_in(jax.random.fold_in(key_of[15], part), 71), part)
    w1_self = bell_draw(key_of[8], (F, H), F ** -0.5, 0.21875, ((0, 4),))
    w1_neigh = bell_draw(key_of[9], (F, H), F ** -0.5, 0.21875, ((0, 4),))
    bias_one = bell_draw(key_of[10], (H,), 0.5, 3.0, (), jnp.float32)
    w2_self = bell_draw(key_of[11], (H, C), H ** -0.5, 0.1875)
    w2_neigh = bell_draw(key_of[12], (H, C), H ** -0.5, 0.1875)
    bias_two = bell_draw(key_of[13], (C,), 0.5, 3.0, (), jnp.float32)
    cotangent = bell_draw(own_keys[14], (SLOTS, NODES, C), 0.01, 0.06, ((0, 4), (1, 4)), jnp.float32)
    return {"features": features, "self_ids": self_ids, "first_dst": first_dst, "first_src": first_src, "first_words": first_words, "second_dst": second_dst, "second_src": second_src, "second_words": second_words, "w1_self": w1_self, "w1_neigh": w1_neigh, "bias_one": bias_one, "w2_self": w2_self, "w2_neigh": w2_neigh, "bias_two": bias_two, "cotangent": cotangent}


highest = lax.Precision.HIGHEST


def unpack_masks(packed_words):
    shifts = jnp.arange(30, dtype=jnp.int32)
    bit_table = jnp.right_shift(packed_words[:, :, None, :], shifts[None, None, :, None]) & 1
    bit_table = bit_table.reshape(packed_words.shape[0], packed_words.shape[1] * 30, packed_words.shape[2])
    return bit_table[:, :BLK, :].astype(jnp.float32)


def block_sums(tile_masks, sources, dst_blocks, block_count):
    products = jnp.einsum("trs,tsw->trw", tile_masks, sources, precision=highest)
    onehot_dst = (dst_blocks[:, None] == jnp.arange(block_count, dtype=jnp.int32)[None, :]).astype(jnp.float32)
    totals = jnp.einsum("td,trw->drw", onehot_dst, products, precision=highest)
    degree = jnp.einsum("td,tr->dr", onehot_dst, jnp.sum(tile_masks, axis=2), precision=highest)
    return totals.reshape(block_count * BLK, -1), degree.reshape(block_count * BLK)


def reference(features, self_ids, first_dst, first_src, first_words, second_dst, second_src, second_words, w1_self, w1_neigh, bias_one, w2_self, w2_neigh, bias_two, cotangent):
    wself_groups = w1_self.reshape(N_FEAT, COLS, H)
    wneigh_groups = w1_neigh.reshape(N_FEAT, COLS, H)

    def one_slot(operands):
        feature_rows, self_rows, dst_one, src_one, words_one, dst_two, src_two, words_two, cot_rows = operands
        first_masks = unpack_masks(words_one)
        source_blocks = feature_rows.reshape(SRC_BLOCKS, BLK, F)[src_one].astype(jnp.float32)
        totals, degree = block_sums(first_masks, source_blocks, dst_one, N_FEAT)
        first_mean = (totals / jnp.maximum(degree, 1.0)[:, None]).astype(jnp.bfloat16)
        self_feats = feature_rows[self_rows]
        self_groups = self_feats.reshape(NODES, N_FEAT, COLS).transpose(1, 0, 2)
        mean_groups = first_mean.reshape(NODES, N_FEAT, COLS).transpose(1, 0, 2)

        def add_group(running, member):
            self_part, mean_part, wself_part, wneigh_part = member
            partial_sum = jnp.dot(self_part, wself_part, preferred_element_type=jnp.float32) + jnp.dot(mean_part, wneigh_part, preferred_element_type=jnp.float32)
            rounded = lax.optimization_barrier(partial_sum.astype(jnp.bfloat16))
            return running + rounded.astype(jnp.float32), None

        summed, _ = lax.scan(add_group, jnp.zeros((NODES, H), jnp.float32), (self_groups, mean_groups, wself_groups, wneigh_groups))
        hidden = jax.nn.relu(summed + bias_one).astype(jnp.bfloat16)
        second_masks = unpack_masks(words_two)
        hidden_blocks = hidden.reshape(N_FEAT, BLK, H)[src_two].astype(jnp.float32)
        totals_two, degree_two = block_sums(second_masks, hidden_blocks, dst_two[:, 0], N_FEAT)
        second_mean = totals_two / jnp.maximum(degree_two, 1.0)[:, None]
        logits = jnp.dot(hidden, w2_self, preferred_element_type=jnp.float32) + jnp.dot(second_mean, w2_neigh.astype(jnp.float32), precision=highest) + bias_two
        grad_self = jnp.dot(hidden.astype(jnp.float32).T, cot_rows, precision=highest)
        grad_neigh = jnp.dot(second_mean.T, cot_rows, precision=highest)
        return logits, grad_self, grad_neigh

    logits, grad_self, grad_neigh = lax.map(one_slot, (features, self_ids, first_dst, first_src, first_words, second_dst, second_src, second_words, cotangent))
    return logits, jnp.sum(grad_self, axis=0), jnp.sum(grad_neigh, axis=0)
```

```python
import functools

import jax
import jax.numpy as jnp
from jax import lax
from jax.experimental import pallas as pl
from jax.experimental.pallas import tpu as pltpu
from jax.sharding import PartitionSpec as P

BLK = 128
WORD = 30
MESH = pl.DeviceIdType.MESH
F32 = jnp.float32
BF16 = jnp.bfloat16


def round_up(value, step):
    return -(-value // step) * step


def each(count, step):
    if count <= 4:
        for index in range(count):
            step(index)
    else:
        lax.fori_loop(0, count, lambda index, carry: (step(index), carry)[1], 0)


def partners(me, size):
    if size & (size - 1) == 0:
        return [me ^ k for k in range(size - 1, 0, -1)]
    return [lax.rem(me + k, size) for k in range(1, size)]


def dot(a, b, dims):
    return lax.dot_general(a, b, (dims, ((), ())), preferred_element_type=F32)


NN = ((1,), (0,))
NT = ((1,), (1,))
TN = ((0,), (0,))


def unpack(words, row_word, row_shift):
    spread = jnp.broadcast_to(words[0:1, :], (BLK, BLK))
    for k in range(1, words.shape[0]):
        spread = jnp.where(row_word == k, words[k : k + 1, :], spread)
    return (jnp.right_shift(spread, row_shift) & 1).astype(F32)


def kernel(
    sizes,
    dst1,
    src1,
    dst2,
    src2,
    ids,
    words1,
    words2,
    feats,
    w1s,
    w1n,
    b1,
    w2s,
    w2n,
    cot,
    logits_out,
    grads_out,
    cotg,
    masks1,
    masks2,
    adj1,
    adj2,
    part,
    got,
    w2z,
    lf,
    lsend,
    lgot,
    cg,
    gsend,
    ggot,
    full,
    cot_s,
    cot_r,
    part_s,
    part_r,
    l_s,
    l_r,
    g_s,
    g_r,
    z_s,
    z_r,
    x_s,
    x_r,
    c_s,
    c_r,
):
    nz, nd, nr, hc, classes = sizes
    z = lax.axis_index("feat")
    d = lax.axis_index("dp")
    r = lax.axis_index("rep")
    y = lax.axis_index("groups")
    q = d * nr + r
    planes = nd * nr
    nodes = nz * BLK
    tile1, tile2 = words1.shape[0], words2.shape[0]
    cp = cot.shape[0]
    pc = gsend.shape[1]
    zs = partners(z, nz)
    qs = partners(q, planes)

    def at(zz, qq):
        return (y, zz, qq // nr, lax.rem(qq, nr))

    def remote(src, dst, send, recv, where):
        return pltpu.make_async_remote_copy(
            src_ref=src, dst_ref=dst, send_sem=send, recv_sem=recv, device_id=where, device_id_type=MESH
        )

    barrier = pltpu.get_barrier_semaphore()
    for p in zs:
        pl.semaphore_signal(barrier, inc=1, device_id=at(p, q), device_id_type=MESH)
    for p in qs:
        pl.semaphore_signal(barrier, inc=1, device_id=at(z, p), device_id_type=MESH)
    pl.semaphore_wait(barrier, nz + planes - 2)

    pending = []

    def send(src, dst, s, rv, where):
        copy = remote(src, dst, s, rv, where)
        copy.start()
        pending.append(copy)

    def arrived(dst, s, rv, where):
        remote(dst, dst, s, rv, where).wait_recv()

    for p in zs:
        send(cot, cotg.at[z], cot_s.at[p], cot_r.at[z], at(p, q))
    cotg[z] = cot[...]

    row = lax.broadcasted_iota(jnp.int32, (BLK, BLK), 0)
    row_word = jnp.zeros((BLK, BLK), jnp.int32)
    for k in range(1, words1.shape[1]):
        row_word = row_word + (row >= WORD * k).astype(jnp.int32)
    row_shift = row - WORD * row_word

    for t in range(tile1):
        masks1[t] = unpack(words1[t], row_word, row_shift)

    def fill1(block):
        for t in range(tile1):
            keep = jnp.where(jnp.full((BLK, BLK), dst1[t], jnp.int32) == block, masks1[t], 0.0)
            adj1[pl.ds(pl.multiple_of(block * BLK, BLK), BLK), t * BLK : (t + 1) * BLK] = keep.astype(BF16)

    each(nz, fill1)
    picked = []
    for t in range(tile1):
        wanted = jnp.full((feats.shape[0], BLK), src1[t], jnp.int32)
        block = feats[:, 0:BLK]
        for k in range(1, feats.shape[1] // BLK):
            block = jnp.where(wanted == k, feats[:, k * BLK : (k + 1) * BLK], block)
        picked.append(block)
    picked = jnp.concatenate(picked, axis=1)
    degree = dot(jnp.ones((16, tile1 * BLK), BF16), adj1[...], NT)[0:1, :]
    mean_t = (dot(picked, adj1[...], NT) / jnp.maximum(degree, 1.0)).astype(BF16)
    sources = feats.shape[1]
    chunk = 512
    self_t = None
    for k in range(0, sources, chunk):
        spot = lax.broadcasted_iota(jnp.int32, (chunk, nodes), 0) + k
        onehot = jnp.where(spot == ids[...], 1.0, 0.0).astype(BF16)
        term = dot(feats[:, k : k + chunk], onehot, NN)
        self_t = term if self_t is None else self_t + term
    self_t = self_t.astype(BF16)
    for j in range(nz):
        cols = slice(j * hc, (j + 1) * hc)
        part[j] = (dot(self_t, w1s[:, cols], TN) + dot(mean_t, w1n[:, cols], TN)).astype(BF16)
    for p in zs:
        send(part.at[p], got.at[z], part_s.at[p], part_r.at[z], at(p, q))

    for t in range(tile2):
        masks2[t] = unpack(words2[t], row_word, row_shift)

    def fill2(dst):
        rows = pl.ds(pl.multiple_of(dst * BLK, BLK), BLK)
        kept = [
            jnp.where(jnp.full((BLK, BLK), dst2[t], jnp.int32) == dst, masks2[t], 0.0)
            for t in range(tile2)
        ]
        for src in range(nz):
            count = jnp.zeros((BLK, BLK), F32)
            for t in range(tile2):
                count = count + jnp.where(jnp.full((BLK, BLK), src2[t], jnp.int32) == src, kept[t], 0.0)
            adj2[rows, src * BLK : (src + 1) * BLK] = count.astype(BF16)

    each(nz, fill2)
    degree2 = jnp.maximum(dot(jnp.ones((16, nodes), BF16), adj2[...], NT)[0:1, :], 1.0)
    inverse2 = 1.0 / degree2
    w2z[...] = jnp.zeros_like(w2z)
    if w2s.shape[1] == hc:
        part_w2s, part_w2n, bias = w2s[...], w2n[...], b1[...]
    else:
        mine = pl.ds(pl.multiple_of(z * hc, BLK), hc)
        part_w2s, part_w2n, bias = w2s[:, mine], w2n[:, mine], b1[:, mine]
    w2z[0:classes, :] = part_w2s.astype(F32)
    w2z[cp : cp + classes, :] = part_w2n.astype(F32)
    w2 = w2z[...].astype(BF16)
    for p in zs:
        arrived(cotg.at[p], cot_s.at[p], cot_r.at[p], at(p, q))
    for j in range(nz):
        cols = slice(j * BLK, (j + 1) * BLK)
        cg[0:cp, cols] = cotg[j]
    scaled = (cg[0:cp, :].astype(F32) * inverse2).astype(BF16)
    cg[cp : 2 * cp, :] = dot(scaled, adj2[...], NN).astype(BF16)
    if cg.shape[0] > 2 * cp:
        cg[2 * cp :, :] = jnp.zeros((cg.shape[0] - 2 * cp, nodes), BF16)

    summed = part[z].astype(F32) + bias
    for p in zs:
        arrived(got.at[p], part_s.at[p], part_r.at[p], at(p, q))
        summed = summed + got[p].astype(F32)
    hidden = jnp.maximum(summed, 0.0).astype(BF16)

    grads = dot(cg[...], hidden, NN).astype(BF16)
    for p in range(planes):
        gsend[p] = grads[p * pc : (p + 1) * pc, :]
    for p in qs:
        send(gsend.at[p], ggot.at[q], g_s.at[p], g_r.at[q], at(z, p))

    uv = dot(w2, hidden, NT)
    lf[...] = uv[0:cp, :] + dot(uv[cp:, :].astype(BF16), adj2[...], NT) * inverse2
    for j in range(nz):
        lsend[j] = lf[:, j * BLK : (j + 1) * BLK].astype(BF16)

    total = gsend[q].astype(F32)
    for p in qs:
        arrived(ggot.at[p], g_s.at[p], g_r.at[p], at(z, p))
        total = total + ggot[p].astype(F32)
    full[z, q] = total.astype(BF16)
    for p in zs:
        send(full.at[z, q], full.at[z, q], z_s.at[p], z_r.at[z], at(p, q))
    for p in zs:
        send(lsend.at[p], lgot.at[z], l_s.at[p], l_r.at[z], at(p, q))

    ds = partners(d, nd)
    rs = partners(r, nr)

    def to_core(zz, dd):
        piece = full.at[zz, dd * nr + r]
        for p in rs:
            send(piece, piece, c_s.at[zz, dd, p], c_r.at[zz, dd, r], (y, z, d, p))

    for zz in [z] + zs[::-1]:
        piece = full.at[zz, q]
        if zz is not z:
            arrived(piece, z_s.at[zz], z_r.at[zz], at(zz, q))
        for p in ds:
            send(piece, piece, x_s.at[zz, p], x_r.at[zz, d], (y, z, p, r))
        to_core(zz, d)
    for zz in [z] + zs[::-1]:
        for p in ds:
            arrived(full.at[zz, p * nr + r], x_s.at[zz, p], x_r.at[zz, p], (y, z, p, r))
            to_core(zz, p)

    out = lf[:, pl.ds(pl.multiple_of(z * BLK, BLK), BLK)]
    for p in zs:
        arrived(lgot.at[p], l_s.at[p], l_r.at[p], at(p, q))
        out = out + lgot[p].astype(F32)
    logits_out[...] = out

    for zz in range(nz):
        for dd in range(nd):
            for p in rs:
                arrived(full.at[zz, dd * nr + p], c_s.at[zz, dd, p], c_r.at[zz, dd, p], (y, z, d, p))
    for zz in range(nz):
        for p in range(planes):
            grads_out[p * pc : (p + 1) * pc, zz * hc : (zz + 1) * hc] = full[zz, p]
    for copy in pending:
        copy.wait_send()


def body(nd, nr, *args):
    (features, self_ids, first_dst, first_src, first_words, second_dst, second_src, second_words) = args[:8]
    w1_self, w1_neigh, bias_one, w2_self, w2_neigh, bias_two, cotangent = args[8:]
    nz = lax.axis_size("feat")
    planes = nd * nr
    h, classes = w2_self.shape
    hc = h // nz
    nodes = self_ids.shape[1]
    tile1, tile2 = first_words.shape[1], second_words.shape[1]
    cp = round_up(classes, 16)
    rows = round_up(2 * cp, 16 * planes)
    pc = rows // planes
    cot = jnp.pad(cotangent[0].T.astype(BF16), ((0, cp - classes), (0, 0)))
    w2s, w2n, b1 = w2_self.T, w2_neigh.T, bias_one[None, :]
    if hc % BLK:
        first = lax.axis_index("feat") * hc
        w2s, w2n, b1 = [lax.dynamic_slice_in_dim(a, first, hc, 1) for a in (w2s, w2n, b1)]
    smem = pl.BlockSpec(memory_space=pltpu.SMEM)
    vmem = pl.BlockSpec(memory_space=pltpu.VMEM)
    dma = pltpu.SemaphoreType.DMA
    logits, grads = pl.pallas_call(
        functools.partial(kernel, (nz, nd, nr, hc, classes)),
        out_shape=(jax.ShapeDtypeStruct((cp, BLK), F32), jax.ShapeDtypeStruct((rows, h), BF16)),
        in_specs=[smem] * 4 + [vmem] * 10,
        out_specs=(vmem, vmem),
        scratch_shapes=[
            pltpu.VMEM((nz, cp, BLK), BF16),
            pltpu.VMEM((tile1, BLK, BLK), F32),
            pltpu.VMEM((tile2, BLK, BLK), F32),
            pltpu.VMEM((nodes, tile1 * BLK), BF16),
            pltpu.VMEM((nodes, nodes), BF16),
            pltpu.VMEM((nz, nodes, hc), BF16),
            pltpu.VMEM((nz, nodes, hc), BF16),
            pltpu.VMEM((2 * cp, hc), F32),
            pltpu.VMEM((cp, nodes), F32),
            pltpu.VMEM((nz, cp, BLK), BF16),
            pltpu.VMEM((nz, cp, BLK), BF16),
            pltpu.VMEM((rows, nodes), BF16),
            pltpu.VMEM((planes, pc, hc), BF16),
            pltpu.VMEM((planes, pc, hc), BF16),
            pltpu.VMEM((nz, planes, pc, hc), BF16),
            dma((nz,)),
            dma((nz,)),
            dma((nz,)),
            dma((nz,)),
            dma((nz,)),
            dma((nz,)),
            dma((planes,)),
            dma((planes,)),
            dma((nz,)),
            dma((nz,)),
            dma((nz, nd)),
            dma((nz, nd)),
            dma((nz, nd, nr)),
            dma((nz, nd, nr)),
        ],
        compiler_params=pltpu.CompilerParams(
            collective_id=0, has_side_effects=True, vmem_limit_bytes=60 * 1024 * 1024
        ),
    )(
        first_dst[0],
        first_src[0],
        second_dst[0, :, 0],
        second_src[0],
        self_ids,
        first_words[0],
        second_words[0],
        features[0].T,
        w1_self,
        w1_neigh,
        b1,
        w2s,
        w2n,
        cot,
    )
    logits = logits[:classes].T + bias_two
    grad_self = grads[:classes].astype(F32).T
    grad_neigh = grads[cp : cp + classes].astype(F32).T
    return (logits[None], grad_self, grad_neigh)


def solution(mesh):
    slot = ("groups", "dp", "rep")
    placed = (
        P(slot, None, "feat"),
        P(slot, None),
        P(slot, None),
        P(slot, None),
        P(slot, None, None, None),
        P(slot, None, None),
        P(slot, None),
        P(slot, None, None, None),
        P("feat", None),
        P("feat", None),
        P(),
        P(),
        P(),
        P(),
        P(slot, "feat", None),
    )
    return jax.shard_map(
        functools.partial(body, mesh.shape["dp"], mesh.shape["rep"]),
        mesh=mesh,
        in_specs=placed,
        out_specs=(P(slot, "feat", None), P("groups", None), P("groups", None)),
        check_vma=False,
    )
```

```python
import functools

import jax
import jax.numpy as jnp
from jax import lax
from jax.experimental import pallas as pl
from jax.experimental.pallas import tpu as pltpu
from jax.sharding import PartitionSpec as P

BLK = 128
WORD = 30
MESH = pl.DeviceIdType.MESH
F32 = jnp.float32
BF16 = jnp.bfloat16


def round_up(value, step):
    return -(-value // step) * step


def each(count, step):
    if count <= 4:
        for index in range(count):
            step(index)
    else:
        lax.fori_loop(0, count, lambda index, carry: (step(index), carry)[1], 0)


def partners(me, size):
    if size & (size - 1) == 0:
        return [me ^ k for k in range(size - 1, 0, -1)]
    return [lax.rem(me + k, size) for k in range(1, size)]


def dot(a, b, dims):
    return lax.dot_general(a, b, (dims, ((), ())), preferred_element_type=F32)


NN = ((1,), (0,))
NT = ((1,), (1,))
TN = ((0,), (0,))


def unpack(words, row_word, row_shift):
    spread = jnp.broadcast_to(words[0], (BLK, BLK))
    for k in range(1, len(words)):
        spread = jnp.where(row_word == k, words[k], spread)
    return (jnp.right_shift(spread, row_shift) & 1).astype(F32)


def kernel(
    sizes,
    dst1,
    src1,
    dst2,
    src2,
    ids,
    words1,
    words2,
    feats,
    w1s,
    w1n,
    b1,
    w2s,
    w2n,
    b2,
    cot,
    logits_out,
    grads_out,
    cotg,
    wide,
    masks1,
    masks2,
    adj1,
    adj2,
    part,
    got,
    w2z,
    lf,
    lsend,
    lgot,
    cg,
    gsend,
    ggot,
    full,
    cot_s,
    cot_r,
    part_s,
    part_r,
    l_s,
    l_r,
    g_s,
    g_r,
    z_s,
    z_r,
    x_s,
    x_r,
    c_s,
    c_r,
):
    nz, nd, nr, hc, classes = sizes
    z = lax.axis_index("feat")
    d = lax.axis_index("dp")
    r = lax.axis_index("rep")
    y = lax.axis_index("groups")
    q = d * nr + r
    planes = nd * nr
    nodes = nz * BLK
    tile1, tile2 = dst1.shape[0], dst2.shape[0]
    per = words1.shape[0] // tile1
    cp = cotg.shape[1]
    pc = gsend.shape[1]
    zs = partners(z, nz)
    qs = partners(q, planes)

    def at(zz, qq):
        return (y, zz, qq // nr, lax.rem(qq, nr))

    def remote(src, dst, send, recv, where):
        return pltpu.make_async_remote_copy(
            src_ref=src, dst_ref=dst, send_sem=send, recv_sem=recv, device_id=where, device_id_type=MESH
        )

    barrier = pltpu.get_barrier_semaphore()
    for p in zs:
        pl.semaphore_signal(barrier, inc=1, device_id=at(p, q), device_id_type=MESH)
    for p in qs:
        pl.semaphore_signal(barrier, inc=1, device_id=at(z, p), device_id_type=MESH)
    wide[...] = jnp.zeros_like(wide)
    wide[0:classes, :] = cot[:, 0, :]
    cotg[z] = wide[...].astype(BF16)
    pl.semaphore_wait(barrier, nz + planes - 2)

    pending = []

    def send(src, dst, s, rv, where):
        copy = remote(src, dst, s, rv, where)
        copy.start()
        pending.append(copy)

    def arrived(dst, s, rv, where):
        remote(dst, dst, s, rv, where).wait_recv()

    for p in zs:
        send(cotg.at[z], cotg.at[z], cot_s.at[p], cot_r.at[z], at(p, q))

    row = lax.broadcasted_iota(jnp.int32, (BLK, BLK), 0)
    row_word = jnp.zeros((BLK, BLK), jnp.int32)
    for k in range(1, per):
        row_word = row_word + (row >= WORD * k).astype(jnp.int32)
    row_shift = row - WORD * row_word

    for t in range(tile1):
        masks1[t] = unpack([words1[t * per + k] for k in range(per)], row_word, row_shift)

    def fill1(block):
        for t in range(tile1):
            keep = jnp.where(jnp.full((BLK, BLK), dst1[t], jnp.int32) == block, masks1[t], 0.0)
            adj1[pl.ds(pl.multiple_of(block * BLK, BLK), BLK), t * BLK : (t + 1) * BLK] = keep.astype(BF16)

    each(nz, fill1)
    picked = []
    for t in range(tile1):
        wanted = jnp.full((feats.shape[0], BLK), src1[t], jnp.int32)
        block = feats[:, 0:BLK]
        for k in range(1, feats.shape[1] // BLK):
            block = jnp.where(wanted == k, feats[:, k * BLK : (k + 1) * BLK], block)
        picked.append(block)
    picked = jnp.concatenate(picked, axis=1)
    degree = dot(jnp.ones((16, tile1 * BLK), BF16), adj1[...], NT)[0:1, :]
    mean_t = (dot(picked, adj1[...], NT) / jnp.maximum(degree, 1.0)).astype(BF16)
    sources = feats.shape[1]
    chunk = 512
    self_t = None
    for k in range(0, sources, chunk):
        spot = lax.broadcasted_iota(jnp.int32, (chunk, nodes), 0) + k
        onehot = jnp.where(spot == ids[...], 1.0, 0.0).astype(BF16)
        term = dot(feats[:, k : k + chunk], onehot, NN)
        self_t = term if self_t is None else self_t + term
    self_t = self_t.astype(BF16)
    for j in range(nz):
        cols = slice(j * hc, (j + 1) * hc)
        part[j] = (dot(self_t, w1s[:, cols], TN) + dot(mean_t, w1n[:, cols], TN)).astype(BF16)
    for p in zs:
        send(part.at[p], got.at[z], part_s.at[p], part_r.at[z], at(p, q))

    for t in range(tile2):
        masks2[t] = unpack([words2[t * per + k] for k in range(per)], row_word, row_shift)

    def fill2(dst):
        rows = pl.ds(pl.multiple_of(dst * BLK, BLK), BLK)
        kept = [
            jnp.where(jnp.full((BLK, BLK), dst2[t], jnp.int32) == dst, masks2[t], 0.0)
            for t in range(tile2)
        ]
        for src in range(nz):
            count = jnp.zeros((BLK, BLK), F32)
            for t in range(tile2):
                count = count + jnp.where(jnp.full((BLK, BLK), src2[t], jnp.int32) == src, kept[t], 0.0)
            adj2[rows, src * BLK : (src + 1) * BLK] = count.astype(BF16)

    each(nz, fill2)
    degree2 = jnp.maximum(dot(jnp.ones((16, nodes), BF16), adj2[...], NT)[0:1, :], 1.0)
    inverse2 = 1.0 / degree2
    w2z[...] = jnp.zeros_like(w2z)
    if w2s.shape[1] == hc:
        part_w2s, part_w2n, bias = w2s[...], w2n[...], b1[...]
    else:
        mine = pl.ds(pl.multiple_of(z * hc, BLK), hc)
        part_w2s, part_w2n, bias = w2s[:, mine], w2n[:, mine], b1[:, mine]
    w2z[0:classes, :] = part_w2s.astype(F32)
    w2z[cp : cp + classes, :] = part_w2n.astype(F32)
    w2 = w2z[...].astype(BF16)
    for p in zs:
        arrived(cotg.at[p], cot_s.at[p], cot_r.at[p], at(p, q))
    for j in range(nz):
        cols = slice(j * BLK, (j + 1) * BLK)
        cg[0:cp, cols] = cotg[j]
    scaled = (cg[0:cp, :].astype(F32) * inverse2).astype(BF16)
    cg[cp : 2 * cp, :] = dot(scaled, adj2[...], NN).astype(BF16)
    if cg.shape[0] > 2 * cp:
        cg[2 * cp :, :] = jnp.zeros((cg.shape[0] - 2 * cp, nodes), BF16)

    summed = part[z].astype(F32) + bias
    for p in zs:
        arrived(got.at[p], part_s.at[p], part_r.at[p], at(p, q))
        summed = summed + got[p].astype(F32)
    hidden = jnp.maximum(summed, 0.0).astype(BF16)

    grads = dot(cg[...], hidden, NN).astype(BF16)
    for p in range(planes):
        gsend[p] = grads[p * pc : (p + 1) * pc, :]
    for p in qs:
        send(gsend.at[p], ggot.at[q], g_s.at[p], g_r.at[q], at(z, p))

    uv = dot(w2, hidden, NT)
    lf[...] = uv[0:cp, :] + dot(uv[cp:, :].astype(BF16), adj2[...], NT) * inverse2
    for j in range(nz):
        lsend[j] = lf[:, j * BLK : (j + 1) * BLK].astype(BF16)

    total = gsend[q].astype(F32)
    for p in qs:
        arrived(ggot.at[p], g_s.at[p], g_r.at[p], at(z, p))
        total = total + ggot[p].astype(F32)
    full[z, q] = total.astype(BF16)
    for p in zs:
        send(full.at[z, q], full.at[z, q], z_s.at[p], z_r.at[z], at(p, q))
    for p in zs:
        send(lsend.at[p], lgot.at[z], l_s.at[p], l_r.at[z], at(p, q))

    ds = partners(d, nd)
    rs = partners(r, nr)

    def to_core(zz, dd):
        piece = full.at[zz, dd * nr + r]
        for p in rs:
            send(piece, piece, c_s.at[zz, dd, p], c_r.at[zz, dd, r], (y, z, d, p))

    for zz in [z] + zs[::-1]:
        piece = full.at[zz, q]
        if zz is not z:
            arrived(piece, z_s.at[zz], z_r.at[zz], at(zz, q))
        for p in ds:
            send(piece, piece, x_s.at[zz, p], x_r.at[zz, d], (y, z, p, r))
        to_core(zz, d)
    for zz in [z] + zs[::-1]:
        for p in ds:
            arrived(full.at[zz, p * nr + r], x_s.at[zz, p], x_r.at[zz, p], (y, z, p, r))
            to_core(zz, p)

    out = lf[:, pl.ds(pl.multiple_of(z * BLK, BLK), BLK)]
    for p in zs:
        arrived(lgot.at[p], l_s.at[p], l_r.at[p], at(p, q))
        out = out + lgot[p].astype(F32)
    wide[...] = out
    bias_two = jnp.broadcast_to(b2[...], (BLK, classes)).T
    logits_out[:, 0, :] = wide[0:classes, :] + bias_two

    for zz in range(nz):
        for dd in range(nd):
            for p in rs:
                arrived(full.at[zz, dd * nr + p], c_s.at[zz, dd, p], c_r.at[zz, dd, p], (y, z, d, p))
    for zz in range(nz):
        for p in range(planes):
            grads_out[p * pc : (p + 1) * pc, zz * hc : (zz + 1) * hc] = full[zz, p]
    for copy in pending:
        copy.wait_send()


def body(nd, nr, *args):
    (features, self_ids, first_dst, first_src, first_words, second_dst, second_src, second_words) = args[:8]
    w1_self, w1_neigh, bias_one, w2_self, w2_neigh, bias_two, cotangent = args[8:]
    nz = lax.axis_size("feat")
    planes = nd * nr
    h, classes = w2_self.shape
    hc = h // nz
    nodes = self_ids.shape[1]
    tile1, tile2 = first_words.shape[1], second_words.shape[1]
    cp = round_up(classes, 16)
    rows = round_up(2 * cp, 16 * planes)
    pc = rows // planes
    cot = cotangent.transpose(2, 0, 1)
    w2s, w2n, b1 = w2_self.T, w2_neigh.T, bias_one[None, :]
    if hc % BLK:
        first = lax.axis_index("feat") * hc
        w2s, w2n, b1 = [lax.dynamic_slice_in_dim(a, first, hc, 1) for a in (w2s, w2n, b1)]
    smem = pl.BlockSpec(memory_space=pltpu.SMEM)
    vmem = pl.BlockSpec(memory_space=pltpu.VMEM)
    dma = pltpu.SemaphoreType.DMA
    logits, grads = pl.pallas_call(
        functools.partial(kernel, (nz, nd, nr, hc, classes)),
        out_shape=(jax.ShapeDtypeStruct((classes, 1, BLK), F32), jax.ShapeDtypeStruct((rows, h), BF16)),
        in_specs=[smem] * 4 + [vmem] * 11,
        out_specs=(vmem, vmem),
        scratch_shapes=[
            pltpu.VMEM((nz, cp, BLK), BF16),
            pltpu.VMEM((cp, BLK), F32),
            pltpu.VMEM((tile1, BLK, BLK), F32),
            pltpu.VMEM((tile2, BLK, BLK), F32),
            pltpu.VMEM((nodes, tile1 * BLK), BF16),
            pltpu.VMEM((nodes, nodes), BF16),
            pltpu.VMEM((nz, nodes, hc), BF16),
            pltpu.VMEM((nz, nodes, hc), BF16),
            pltpu.VMEM((2 * cp, hc), F32),
            pltpu.VMEM((cp, nodes), F32),
            pltpu.VMEM((nz, cp, BLK), BF16),
            pltpu.VMEM((nz, cp, BLK), BF16),
            pltpu.VMEM((rows, nodes), BF16),
            pltpu.VMEM((planes, pc, hc), BF16),
            pltpu.VMEM((planes, pc, hc), BF16),
            pltpu.VMEM((nz, planes, pc, hc), BF16),
            dma((nz,)),
            dma((nz,)),
            dma((nz,)),
            dma((nz,)),
            dma((nz,)),
            dma((nz,)),
            dma((planes,)),
            dma((planes,)),
            dma((nz,)),
            dma((nz,)),
            dma((nz, nd)),
            dma((nz, nd)),
            dma((nz, nd, nr)),
            dma((nz, nd, nr)),
        ],
        compiler_params=pltpu.CompilerParams(
            collective_id=0, has_side_effects=True, vmem_limit_bytes=60 * 1024 * 1024
        ),
    )(
        first_dst[0],
        first_src[0],
        second_dst[0, :, 0],
        second_src[0],
        self_ids,
        first_words[0].reshape(-1, 1, BLK),
        second_words[0].reshape(-1, 1, BLK),
        features[0].T,
        w1_self,
        w1_neigh,
        b1,
        w2s,
        w2n,
        bias_two[None, :],
        cot,
    )
    logits = logits.transpose(1, 2, 0)
    grad_self = grads[:classes].astype(F32).T
    grad_neigh = grads[cp : cp + classes].astype(F32).T
    return (logits, grad_self, grad_neigh)


def solution(mesh):
    slot = ("groups", "dp", "rep")
    placed = (
        P(slot, None, "feat"),
        P(slot, None),
        P(slot, None),
        P(slot, None),
        P(slot, None, None, None),
        P(slot, None, None),
        P(slot, None),
        P(slot, None, None, None),
        P("feat", None),
        P("feat", None),
        P(),
        P(),
        P(),
        P(),
        P(slot, "feat", None),
    )
    return jax.shard_map(
        functools.partial(body, mesh.shape["dp"], mesh.shape["rep"]),
        mesh=mesh,
        in_specs=placed,
        out_specs=(P(slot, "feat", None), P("groups", None), P("groups", None)),
        check_vma=False,
    )
```

```python
import functools

import jax
import jax.numpy as jnp
from jax import lax
from jax.experimental import pallas as pl
from jax.experimental.pallas import tpu as pltpu
from jax.sharding import PartitionSpec as P

BLK = 128
WORD = 30
MESH = pl.DeviceIdType.MESH
F32 = jnp.float32
BF16 = jnp.bfloat16


def round_up(value, step):
    return -(-value // step) * step


def each(count, step):
    if count <= 4:
        for index in range(count):
            step(index)
    else:
        lax.fori_loop(0, count, lambda index, carry: (step(index), carry)[1], 0)


def partners(me, size):
    if size & (size - 1) == 0:
        return [me ^ k for k in range(size - 1, 0, -1)]
    return [lax.rem(me + k, size) for k in range(1, size)]


def dot(a, b, dims):
    return lax.dot_general(a, b, (dims, ((), ())), preferred_element_type=F32)


NN = ((1,), (0,))
NT = ((1,), (1,))
TN = ((0,), (0,))


def unpack(words, row_word, row_shift):
    spread = jnp.broadcast_to(words[0], (BLK, BLK))
    for k in range(1, len(words)):
        spread = jnp.where(row_word == k, words[k], spread)
    return (jnp.right_shift(spread, row_shift) & 1).astype(F32)


def kernel(
    sizes,
    dst1,
    src1,
    dst2,
    src2,
    ids,
    words1,
    words2,
    feats,
    w1s,
    w1n,
    b1,
    w2s,
    w2n,
    b2,
    cot,
    logits_out,
    grads_out,
    cotg,
    wide,
    masks1,
    masks2,
    adj1,
    adj2,
    part,
    got,
    w2z,
    lf,
    lsend,
    lgot,
    cg,
    gsend,
    ggot,
    full,
    cot_s,
    cot_r,
    part_s,
    part_r,
    l_s,
    l_r,
    g_s,
    g_r,
    z_s,
    z_r,
    x_s,
    x_r,
    c_s,
    c_r,
):
    nz, nd, nr, hc, classes = sizes
    z = lax.axis_index("feat")
    d = lax.axis_index("dp")
    r = lax.axis_index("rep")
    y = lax.axis_index("groups")
    q = d * nr + r
    planes = nd * nr
    nodes = nz * BLK
    tile1, tile2 = dst1.shape[0], dst2.shape[0]
    per = words1.shape[0] // tile1
    cp = cotg.shape[1]
    halves, _, pc, hw = gsend.shape
    zs = partners(z, nz)
    qs = partners(q, planes)

    def at(zz, qq):
        return (y, zz, qq // nr, lax.rem(qq, nr))

    def remote(src, dst, send, recv, where):
        return pltpu.make_async_remote_copy(
            src_ref=src, dst_ref=dst, send_sem=send, recv_sem=recv, device_id=where, device_id_type=MESH
        )

    barrier = pltpu.get_barrier_semaphore()
    for p in zs:
        pl.semaphore_signal(barrier, inc=1, device_id=at(p, q), device_id_type=MESH)
    for p in qs:
        pl.semaphore_signal(barrier, inc=1, device_id=at(z, p), device_id_type=MESH)
    wide[...] = jnp.zeros_like(wide)
    wide[0:classes, :] = cot[:, 0, :]
    cotg[z] = wide[...].astype(BF16)
    pl.semaphore_wait(barrier, nz + planes - 2)

    pending = []

    def send(src, dst, s, rv, where):
        copy = remote(src, dst, s, rv, where)
        copy.start()
        pending.append(copy)

    def arrived(dst, s, rv, where):
        remote(dst, dst, s, rv, where).wait_recv()

    for p in zs:
        send(cotg.at[z], cotg.at[z], cot_s.at[p], cot_r.at[z], at(p, q))

    row = lax.broadcasted_iota(jnp.int32, (BLK, BLK), 0)
    row_word = jnp.zeros((BLK, BLK), jnp.int32)
    for k in range(1, per):
        row_word = row_word + (row >= WORD * k).astype(jnp.int32)
    row_shift = row - WORD * row_word

    for t in range(tile1):
        masks1[t] = unpack([words1[t * per + k] for k in range(per)], row_word, row_shift)

    def fill1(block):
        for t in range(tile1):
            keep = jnp.where(jnp.full((BLK, BLK), dst1[t], jnp.int32) == block, masks1[t], 0.0)
            adj1[pl.ds(pl.multiple_of(block * BLK, BLK), BLK), t * BLK : (t + 1) * BLK] = keep.astype(BF16)

    each(nz, fill1)
    picked = []
    for t in range(tile1):
        wanted = jnp.full((feats.shape[0], BLK), src1[t], jnp.int32)
        block = feats[:, 0:BLK]
        for k in range(1, feats.shape[1] // BLK):
            block = jnp.where(wanted == k, feats[:, k * BLK : (k + 1) * BLK], block)
        picked.append(block)
    picked = jnp.concatenate(picked, axis=1)
    degree = dot(jnp.ones((16, tile1 * BLK), BF16), adj1[...], NT)[0:1, :]
    mean_t = (dot(picked, adj1[...], NT) / jnp.maximum(degree, 1.0)).astype(BF16)
    sources = feats.shape[1]
    chunk = 512
    self_t = None
    for k in range(0, sources, chunk):
        spot = lax.broadcasted_iota(jnp.int32, (chunk, nodes), 0) + k
        onehot = jnp.where(spot == ids[...], 1.0, 0.0).astype(BF16)
        term = dot(feats[:, k : k + chunk], onehot, NN)
        self_t = term if self_t is None else self_t + term
    self_t = self_t.astype(BF16)
    for h in range(halves):
        for j in range(nz):
            cols = slice(j * hc + h * hw, j * hc + (h + 1) * hw)
            part[h, j] = (dot(self_t, w1s[:, cols], TN) + dot(mean_t, w1n[:, cols], TN)).astype(BF16)
        for p in zs:
            send(part.at[h, p], got.at[h, z], part_s.at[h, p], part_r.at[h, z], at(p, q))

    for t in range(tile2):
        masks2[t] = unpack([words2[t * per + k] for k in range(per)], row_word, row_shift)

    def fill2(dst):
        rows = pl.ds(pl.multiple_of(dst * BLK, BLK), BLK)
        kept = [
            jnp.where(jnp.full((BLK, BLK), dst2[t], jnp.int32) == dst, masks2[t], 0.0)
            for t in range(tile2)
        ]
        for src in range(nz):
            count = jnp.zeros((BLK, BLK), F32)
            for t in range(tile2):
                count = count + jnp.where(jnp.full((BLK, BLK), src2[t], jnp.int32) == src, kept[t], 0.0)
            adj2[rows, src * BLK : (src + 1) * BLK] = count.astype(BF16)

    each(nz, fill2)
    degree2 = jnp.maximum(dot(jnp.ones((16, nodes), BF16), adj2[...], NT)[0:1, :], 1.0)
    inverse2 = 1.0 / degree2
    w2z[...] = jnp.zeros_like(w2z)
    if w2s.shape[1] == hc:
        part_w2s, part_w2n, bias = w2s[...], w2n[...], b1[...]
    else:
        mine = pl.ds(pl.multiple_of(z * hc, BLK), hc)
        part_w2s, part_w2n, bias = w2s[:, mine], w2n[:, mine], b1[:, mine]
    w2z[0:classes, :] = part_w2s.astype(F32)
    w2z[cp : cp + classes, :] = part_w2n.astype(F32)
    w2 = w2z[...].astype(BF16)
    for p in zs:
        arrived(cotg.at[p], cot_s.at[p], cot_r.at[p], at(p, q))
    for j in range(nz):
        cols = slice(j * BLK, (j + 1) * BLK)
        cg[0:cp, cols] = cotg[j]
    scaled = (cg[0:cp, :].astype(F32) * inverse2).astype(BF16)
    cg[cp : 2 * cp, :] = dot(scaled, adj2[...], NN).astype(BF16)
    if cg.shape[0] > 2 * cp:
        cg[2 * cp :, :] = jnp.zeros((cg.shape[0] - 2 * cp, nodes), BF16)

    ds = partners(d, nd)
    rs = partners(r, nr)

    def multiply(h):
        cols = slice(h * hw, (h + 1) * hw)
        summed = part[h, z].astype(F32) + bias[:, cols]
        for p in zs:
            arrived(got.at[h, p], part_s.at[h, p], part_r.at[h, p], at(p, q))
            summed = summed + got[h, p].astype(F32)
        hidden = jnp.maximum(summed, 0.0).astype(BF16)
        grads = dot(cg[...], hidden, NN).astype(BF16)
        for p in range(planes):
            gsend[h, p] = grads[p * pc : (p + 1) * pc, :]
        for p in qs:
            send(gsend.at[h, p], ggot.at[h, q], g_s.at[h, p], g_r.at[h, q], at(z, p))
        return dot(w2[:, cols], hidden, NT)

    def add_slots(h):
        total = gsend[h, q].astype(F32)
        for p in qs:
            arrived(ggot.at[h, p], g_s.at[h, p], g_r.at[h, p], at(z, p))
            total = total + ggot[h, p].astype(F32)
        full[h, z, q] = total.astype(BF16)
        for p in zs:
            send(full.at[h, z, q], full.at[h, z, q], z_s.at[h, p], z_r.at[h, z], at(p, q))

    def to_core(h, zz, dd):
        piece = full.at[h, zz, dd * nr + r]
        for p in rs:
            send(piece, piece, c_s.at[h, zz, dd, p], c_r.at[h, zz, dd, r], (y, z, d, p))

    def pass_on(h):
        for zz in [z] + zs[::-1]:
            piece = full.at[h, zz, q]
            if zz is not z:
                arrived(piece, z_s.at[h, zz], z_r.at[h, zz], at(zz, q))
            for p in ds:
                send(piece, piece, x_s.at[h, zz, p], x_r.at[h, zz, d], (y, z, p, r))
            to_core(h, zz, d)

    def pass_cores(h):
        for zz in [z] + zs[::-1]:
            for p in ds:
                arrived(full.at[h, zz, p * nr + r], x_s.at[h, zz, p], x_r.at[h, zz, p], (y, z, p, r))
                to_core(h, zz, p)

    uv = multiply(0)
    for h in range(1, halves):
        add_slots(h - 1)
        uv = uv + multiply(h)
    lf[...] = uv[0:cp, :] + dot(uv[cp:, :].astype(BF16), adj2[...], NT) * inverse2
    for j in range(nz):
        lsend[j] = lf[:, j * BLK : (j + 1) * BLK].astype(BF16)
    for p in zs:
        send(lsend.at[p], lgot.at[z], l_s.at[p], l_r.at[z], at(p, q))
    add_slots(halves - 1)
    for h in range(halves):
        pass_on(h)
    for h in range(halves):
        pass_cores(h)

    out = lf[:, pl.ds(pl.multiple_of(z * BLK, BLK), BLK)]
    for p in zs:
        arrived(lgot.at[p], l_s.at[p], l_r.at[p], at(p, q))
        out = out + lgot[p].astype(F32)
    wide[...] = out
    bias_two = jnp.broadcast_to(b2[...], (BLK, classes)).T
    logits_out[:, 0, :] = wide[0:classes, :] + bias_two

    for h in range(halves):
        for zz in range(nz):
            for dd in range(nd):
                for p in rs:
                    arrived(
                        full.at[h, zz, dd * nr + p], c_s.at[h, zz, dd, p], c_r.at[h, zz, dd, p], (y, z, d, p)
                    )
            for p in range(planes):
                first = zz * hc + h * hw
                grads_out[p * pc : (p + 1) * pc, first : first + hw] = full[h, zz, p]
    for copy in pending:
        copy.wait_send()


def body(nd, nr, *args):
    (features, self_ids, first_dst, first_src, first_words, second_dst, second_src, second_words) = args[:8]
    w1_self, w1_neigh, bias_one, w2_self, w2_neigh, bias_two, cotangent = args[8:]
    nz = lax.axis_size("feat")
    planes = nd * nr
    h, classes = w2_self.shape
    hc = h // nz
    nodes = self_ids.shape[1]
    tile1, tile2 = first_words.shape[1], second_words.shape[1]
    cp = round_up(classes, 16)
    rows = round_up(2 * cp, 16 * planes)
    pc = rows // planes
    halves = 1 if hc % (2 * BLK) else 2
    hw = hc // halves
    cot = cotangent.transpose(2, 0, 1)
    w2s, w2n, b1 = w2_self.T, w2_neigh.T, bias_one[None, :]
    if hc % BLK:
        first = lax.axis_index("feat") * hc
        w2s, w2n, b1 = [lax.dynamic_slice_in_dim(a, first, hc, 1) for a in (w2s, w2n, b1)]
    smem = pl.BlockSpec(memory_space=pltpu.SMEM)
    vmem = pl.BlockSpec(memory_space=pltpu.VMEM)
    dma = pltpu.SemaphoreType.DMA
    logits, grads = pl.pallas_call(
        functools.partial(kernel, (nz, nd, nr, hc, classes)),
        out_shape=(jax.ShapeDtypeStruct((classes, 1, BLK), F32), jax.ShapeDtypeStruct((rows, h), BF16)),
        in_specs=[smem] * 4 + [vmem] * 11,
        out_specs=(vmem, vmem),
        scratch_shapes=[
            pltpu.VMEM((nz, cp, BLK), BF16),
            pltpu.VMEM((cp, BLK), F32),
            pltpu.VMEM((tile1, BLK, BLK), F32),
            pltpu.VMEM((tile2, BLK, BLK), F32),
            pltpu.VMEM((nodes, tile1 * BLK), BF16),
            pltpu.VMEM((nodes, nodes), BF16),
            pltpu.VMEM((halves, nz, nodes, hw), BF16),
            pltpu.VMEM((halves, nz, nodes, hw), BF16),
            pltpu.VMEM((2 * cp, hc), F32),
            pltpu.VMEM((cp, nodes), F32),
            pltpu.VMEM((nz, cp, BLK), BF16),
            pltpu.VMEM((nz, cp, BLK), BF16),
            pltpu.VMEM((rows, nodes), BF16),
            pltpu.VMEM((halves, planes, pc, hw), BF16),
            pltpu.VMEM((halves, planes, pc, hw), BF16),
            pltpu.VMEM((halves, nz, planes, pc, hw), BF16),
            dma((nz,)),
            dma((nz,)),
            dma((halves, nz)),
            dma((halves, nz)),
            dma((nz,)),
            dma((nz,)),
            dma((halves, planes)),
            dma((halves, planes)),
            dma((halves, nz)),
            dma((halves, nz)),
            dma((halves, nz, nd)),
            dma((halves, nz, nd)),
            dma((halves, nz, nd, nr)),
            dma((halves, nz, nd, nr)),
        ],
        compiler_params=pltpu.CompilerParams(
            collective_id=0, has_side_effects=True, vmem_limit_bytes=60 * 1024 * 1024
        ),
    )(
        first_dst[0],
        first_src[0],
        second_dst[0, :, 0],
        second_src[0],
        self_ids,
        first_words[0].reshape(-1, 1, BLK),
        second_words[0].reshape(-1, 1, BLK),
        features[0].T,
        w1_self,
        w1_neigh,
        b1,
        w2s,
        w2n,
        bias_two[None, :],
        cot,
    )
    logits = logits.transpose(1, 2, 0)
    grad_self = grads[:classes].astype(F32).T
    grad_neigh = grads[cp : cp + classes].astype(F32).T
    return (logits, grad_self, grad_neigh)


def solution(mesh):
    slot = ("groups", "dp", "rep")
    placed = (
        P(slot, None, "feat"),
        P(slot, None),
        P(slot, None),
        P(slot, None),
        P(slot, None, None, None),
        P(slot, None, None),
        P(slot, None),
        P(slot, None, None, None),
        P("feat", None),
        P("feat", None),
        P(),
        P(),
        P(),
        P(),
        P(slot, "feat", None),
    )
    return jax.shard_map(
        functools.partial(body, mesh.shape["dp"], mesh.shape["rep"]),
        mesh=mesh,
        in_specs=placed,
        out_specs=(P(slot, "feat", None), P("groups", None), P("groups", None)),
        check_vma=False,
    )
```
